32 devices in a mesh: site: 8 (over y, x, core), tm: 4 (over z).
Axes of the slice: x: 2, y: 2, z: 4, core: 2. Of those that a mesh axis runs over, the one named last changes fastest.
Arguments:
- site_field: bfloat16 [32768, 1024], P('site', 'tm'), may hold values from -3 to 3
- positions: bfloat16 [2, 32768], P(None, 'site'), may hold values from 0 to 4
- site_scale: bfloat16 [32768], P('site'), may hold values from 0.5 to 2
- neighbor_blocks: int32 [256, 16], P('site'), may hold values from 0 to 255, as said below
- neighbor_count: int32 [256], P('site'), may hold values from 1 to 16, as said below
- lag_values: float32 [65], replicated, may hold values from 0.05 to 0.25
- time_band: int32 [1024], replicated, may hold values from 1 to 64, as said below
Outputs:
- product: bfloat16 [32768, 1024], P('site', 'tm')
The draws below stay inside these ranges and needn't reach their ends.
Inputs may be any that keep to these rules, and one draw needn't show every extreme that they name: `neighbor_blocks`: block b lies on device b // 32 of the site axis. A block that lists a block of another device names one of the 2 blocks of that device nearest to its own: those with the lowest indices within it when that device comes later along the axis, the highest when it comes earlier. On every device the first block's first 2 slots name all 2 such blocks of the next device (of the first device, for the last). Slots from neighbor_count onward are unused. The first block of every device uses all 16. `time_band`: some time step has 64.
All inputs are finite; a program needn't handle non-finite values.
Results may differ from the reference program's by a relative error of at most 0.0062.
Values may be sent and summed in bfloat16 or wider, within the bound.
A program may use at most 64 MiB of HBM per device.

```python
import math
import jax
import jax.numpy as jnp
from jax import lax

BS = 128
SB_DEV = 32
TIME_DEV = 256
KNB = 16
CAP = 2
BMAX = 64
NBLK = 256
SITES = 32768
TIMES = 1024


def draw_neighbor_blocks(key, part):
    site_total = NBLK // SB_DEV
    key_local, key_side, key_peer, key_window = jax.random.split(key, 4)
    block_ids = jnp.arange(NBLK, dtype=jnp.int32)[:, None]
    owner_site = block_ids // SB_DEV
    local_pick = jax.random.randint(key_local, (NBLK, KNB), 0, SB_DEV)
    hop_count = jax.random.randint(key_peer, (NBLK, KNB), 1, site_total)
    peer_site = (owner_site + hop_count) % site_total
    window_slot = jax.random.randint(key_window, (NBLK, KNB), 0, CAP)
    remote = peer_site * SB_DEV + jnp.where(peer_site > owner_site, window_slot, SB_DEV - CAP + window_slot)
    choose = jax.random.randint(key_side, (NBLK, KNB), 0, 2)
    picked = jnp.where(choose == 0, owner_site * SB_DEV + local_pick, remote)
    column = jnp.arange(KNB, dtype=jnp.int32)[None, :]
    forced_slot = (block_ids % SB_DEV == 0) & (column < CAP)
    next_site = (owner_site + 1) % site_total
    forced = next_site * SB_DEV + jnp.where(next_site > owner_site, column, SB_DEV - CAP + column)
    return jnp.where(forced_slot, forced, picked).astype(jnp.int32)


def draw_neighbor_count(key, part):
    site_total = NBLK // SB_DEV
    key_limit, key_count = jax.random.split(key, 2)
    load_limit = jax.random.randint(key_limit, (site_total, 1), 1, KNB + 1)
    raw_counts = jax.random.randint(key_count, (site_total, SB_DEV), 0, KNB * KNB)
    counts = raw_counts % load_limit + 1
    first_block = jnp.arange(SB_DEV, dtype=jnp.int32)[None, :] == 0
    counts = jnp.where(first_block, KNB, counts)
    return counts.reshape(NBLK).astype(jnp.int32)


def draw_time_band(key, part):
    band_draw = jax.random.randint(key, (TIMES,), 1, BMAX + 1)
    forced_step = jnp.arange(TIMES, dtype=jnp.int32) == TIME_DEV - 1
    return jnp.where(forced_step, BMAX, band_draw).astype(jnp.int32)


def steps_of(own_key, shape, cuts, least, top_value):
    def one(dim, parts):
        heights = jax.random.uniform(jax.random.fold_in(jax.random.fold_in(own_key, 6), dim), (parts,), jnp.float32, least / len(cuts), top_value / len(cuts))
        return jnp.repeat(jnp.exp(heights), shape[dim] // parts).reshape((-1,) + (1,) * (len(shape) - dim - 1))

    factor_of = one(*cuts[0])
    for cut in cuts[1:]:
        factor_of = factor_of * one(*cut)
    return factor_of


def bell_draw(rng, extent, spread, reach, cuts=(), kind=jnp.bfloat16):
    values = spread * jax.random.normal(rng, extent, jnp.float32)
    if cuts:
        values = values * steps_of(rng, extent, cuts, -0.22, 0.18)
    return jnp.clip(values, -reach, reach).astype(kind)


def setup_inputs(seed: int = 0) -> dict:
    key_list = jax.random.split(jax.random.key(seed), 8)
    return {
        "site_field": bell_draw(key_list[0], (SITES, TIMES), 0.5, 3.0, ((0, 8), (1, 4))),
        "positions": jnp.clip(4.0 * jax.random.uniform(key_list[1], (2, SITES), jnp.float32) ** steps_of(key_list[1], (2, SITES), ((1, 8),), -0.2, 0.2), 0.0, 4.0).astype(jnp.bfloat16),
        "site_scale": jnp.clip(jnp.exp(math.log(2.0) - 1.3862944 * jax.random.uniform(key_list[2], (SITES,), jnp.float32) ** steps_of(key_list[2], (SITES,), ((0, 8),), -0.2, 0.2)), 0.5, 2.0).astype(jnp.bfloat16),
        "neighbor_blocks": draw_neighbor_blocks(jax.random.fold_in(key_list[7], 71), 0),
        "neighbor_count": draw_neighbor_count(jax.random.fold_in(key_list[7], 71), 0),
        "lag_values": jnp.clip(jnp.exp(jax.random.uniform(key_list[5], (BMAX + 1,), jnp.float32, math.log(0.05), math.log(0.25))), 0.05, 0.25),
        "time_band": draw_time_band(jax.random.fold_in(key_list[7], 71), 0),
    }


def kernel_tiles(row_geo, col_geo):
    row_geo = row_geo.astype(jnp.float32)
    col_geo = col_geo.astype(jnp.float32)
    across = row_geo[..., 0, :, None] - col_geo[..., 0, None, :]
    upward = row_geo[..., 1, :, None] - col_geo[..., 1, None, :]
    distance = jnp.sqrt(across * across + upward * upward)
    scaled = distance / 3.0
    tapering = jnp.maximum(1.0 - scaled, 0.0) ** 4 * (1.0 + 4.0 * scaled)
    return row_geo[..., 2, :, None] * col_geo[..., 2, None, :] * jnp.exp(distance * -5.0) * tapering

def lag_table(lag_values, row_band, col_band, offset):
    row_total = row_band.shape[-1]
    column_total = col_band.shape[-1]
    span_total = row_total + column_total - 1
    shifts = jnp.arange(span_total, dtype=jnp.int32) - (column_total - 1) - offset
    lag_series = jnp.abs(shifts)
    levels = jnp.arange(lag_values.shape[0], dtype=jnp.int32)
    series = lax.optimization_barrier(jnp.sum(jnp.where(lag_series[:, None] == levels[None, :], lag_values[None, :], 0.0), axis=1))
    repeated = jnp.tile(series, row_total + 1)[:row_total * (span_total + 1)].reshape(row_total, span_total + 1)
    values = repeated[:, :column_total][:, ::-1]
    lag_grid = jnp.abs(jnp.arange(row_total, dtype=jnp.int32)[:, None] - offset - jnp.arange(column_total, dtype=jnp.int32)[None, :])
    band_limit = jnp.minimum(row_band[..., :, None], col_band[..., None, :])
    return jnp.where(lag_grid <= band_limit, values, 0.0).astype(jnp.bfloat16)

def space_product(site_field, positions, site_scale, neighbor_blocks, neighbor_count):
    block_total = neighbor_count.shape[0]
    time_total = site_field.shape[1]
    blocks = site_field.reshape(block_total, BS, time_total)
    geometry = jnp.stack([positions[0], positions[1], site_scale]).reshape(3, block_total, BS).transpose(1, 0, 2)
    slot_live = jnp.arange(KNB, dtype=jnp.int32)[None, :] < neighbor_count[:, None]
    group_total = block_total // SB_DEV

    def one_group(members):
        slot_blocks, live_slots, own_geo = members
        kernel_block = kernel_tiles(own_geo[:, None], geometry[slot_blocks])
        kernel_block = jnp.where(live_slots[:, :, None, None], kernel_block, 0.0).astype(jnp.bfloat16)
        gathered = blocks[slot_blocks]
        summed = jnp.einsum('gkij,gkjt->git', kernel_block.astype(jnp.float32), gathered.astype(jnp.float32))
        return summed.astype(jnp.bfloat16)
    result = lax.map(one_group, (neighbor_blocks.reshape(group_total, SB_DEV, KNB), slot_live.reshape(group_total, SB_DEV, KNB), geometry.reshape(group_total, SB_DEV, 3, BS)))
    return result.reshape(block_total * BS, time_total)

def time_product(space_field, lag_values, time_band):
    site_total, time_total = space_field.shape
    block_width = TIME_DEV
    block_total = time_total // block_width
    padded = jnp.pad(space_field, ((0, 0), (block_width, block_width)))
    band_rows = jnp.pad(time_band, (block_width, block_width)).reshape(block_total + 2, block_width)
    row_band = jnp.concatenate([band_rows[:-2], band_rows[1:-1], band_rows[2:]], axis=1)
    col_band = time_band.reshape(block_total, block_width)
    band_table = lag_table(lag_values, row_band, col_band, block_width)

    def one_block(block_index):
        window = lax.dynamic_slice_in_dim(padded, block_index * block_width, 3 * block_width, 1)
        return jnp.dot(window, band_table[block_index], preferred_element_type=jnp.float32)
    pieces = lax.map(one_block, jnp.arange(block_total, dtype=jnp.int32))
    return pieces.transpose(1, 0, 2).reshape(site_total, time_total).astype(jnp.bfloat16)

def reference(site_field, positions, site_scale, neighbor_blocks, neighbor_count, lag_values, time_band):
    space_field = space_product(site_field, positions, site_scale, neighbor_blocks, neighbor_count)
    return time_product(space_field, lag_values, time_band)
```

```python
import functools
import math

import jax
import jax.numpy as jnp
from jax import lax
from jax.experimental import pallas as pl
from jax.experimental.pallas import tpu as pltpu
from jax.sharding import PartitionSpec as P

CAP = 2
MESH = pl.DeviceIdType.MESH
f32 = jnp.float32
bf16 = jnp.bfloat16


def table_kernel(series_ref, band_ref, mid_ref, halo_ref):
    width = mid_ref.shape[0]
    reach = halo_ref.shape[1] // 2
    total = width + 2 * reach
    base = jnp.broadcast_to(series_ref[...], (total, series_ref.shape[1]))
    values = pltpu.roll(base, 0, 1, stride=1, stride_axis=0)[:, :width]
    turned = jnp.transpose(band_ref[...])
    columns = jnp.concatenate(
        [jnp.broadcast_to(turned[:, j : j + 1], (128, width)) for j in range(total // 128)]
    )
    row = jnp.concatenate([band_ref[pl.ds(total // 128 + j, 1), :] for j in range(width // 128)], 1)
    lag = jnp.abs(
        lax.broadcasted_iota(jnp.int32, (total, width), 0)
        - reach
        - lax.broadcasted_iota(jnp.int32, (total, width), 1)
    ).astype(f32)
    table = jnp.where(lag <= jnp.minimum(columns, row), values, 0.0).astype(bf16)
    first, last = table[:reach], table[reach + width :]
    mid_ref[...] = table[reach : reach + width]
    halo_ref[0] = jnp.concatenate([first, last])
    halo_ref[1] = jnp.concatenate([last, first])


def exchange_kernel(
    site_total, time_total, field, mid, halo, places, scale, pool, geo,
    to_right, to_left, from_left, from_right, scales, edges,
    zsend, zrecv, gsend, grecv, psend, precv,
):
    site, step = lax.axis_index("site"), lax.axis_index("tm")
    rows, width = field.shape
    blocks = scale.shape[0]
    size = rows // blocks
    group = CAP * size
    chunks = rows // (2 * group)
    reach = width // 4
    owned = 2 * blocks

    barrier = pltpu.get_barrier_semaphore()
    for o in range(1, site_total):
        pl.semaphore_signal(
            barrier, inc=1, device_id={"site": lax.rem(site + o, site_total)}, device_id_type=MESH
        )

    for shift in (1, time_total - 1):
        pl.semaphore_signal(
            barrier, inc=1, device_id={"tm": lax.rem(step + shift, time_total)}, device_id_type=MESH
        )

    lane = lax.broadcasted_iota(jnp.int32, (group, 128), 1) < reach

    def pack(c):
        here = pl.ds(pl.multiple_of(c * group, group), group)
        there = pl.ds(pl.multiple_of(rows - (c + 1) * group, group), group)
        right_a = field[here, pl.ds(width - 128, 128)].astype(f32)
        right_b = field[there, pl.ds(width - 128, 128)].astype(f32)
        left_a = field[here, pl.ds(0, 128)].astype(f32)
        left_b = field[there, pl.ds(0, 128)].astype(f32)
        to_right[here, :] = jnp.where(lane, pltpu.roll(right_a, 64, 1), right_b).astype(bf16)
        to_left[here, :] = jnp.where(lane, left_b, pltpu.roll(left_a, 64, 1)).astype(bf16)

    pack(0)
    for k in range(2):
        start = k * (blocks - CAP)
        for j in range(2):
            edges[k, pl.ds(j * CAP, CAP), :] = places[pl.ds(j * blocks + start, CAP), :]
        edges[k, pl.ds(2 * CAP, 8 - 2 * CAP), :] = jnp.zeros((8 - 2 * CAP, 128), f32)

    pl.semaphore_wait(barrier, site_total + 1)

    pieces = [(0, 1), (1, chunks // 2), (chunks // 2, chunks)]

    def sideways(n, right):
        first, last = pieces[n]
        span = pl.ds(first * group, (last - first) * group)
        way = 0 if right else 1
        return pltpu.make_async_remote_copy(
            src_ref=(to_right if right else to_left).at[span],
            dst_ref=(from_left if right else from_right).at[span],
            send_sem=zsend.at[way, n],
            recv_sem=zrecv.at[way, n],
            device_id={"tm": (step + 1) if right else (step - 1)},
            device_id_type=MESH,
        )

    def send(n):
        @pl.when(step < time_total - 1)
        def _():
            sideways(n, True).start()

        @pl.when(step > 0)
        def _():
            sideways(n, False).start()

    def receive(n):
        @pl.when(step > 0)
        def _():
            sideways(n, True).wait_recv()

        @pl.when(step < time_total - 1)
        def _():
            sideways(n, False).wait_recv()

    send(0)

    def points(o):
        later = 1 - (site + o) // site_total
        return pltpu.make_async_remote_copy(
            src_ref=edges.at[later],
            dst_ref=geo.at[pl.ds(owned + 8 * site, 8)],
            send_sem=psend.at[o - 1],
            recv_sem=precv.at[o - 1],
            device_id={"site": lax.rem(site + o, site_total)},
            device_id_type=MESH,
        )

    for o in range(1, site_total):
        points(o).start()

    for n in range(1, len(pieces)):
        lax.fori_loop(pieces[n][0], pieces[n][1], lambda c, _: (pack(c), 0)[1], 0)
        send(n)

    geo[pl.ds(0, owned), :] = places[...]

    @pl.when(step == 0)
    def _():
        from_left[...] = jnp.zeros_like(from_left)

    @pl.when(step == time_total - 1)
    def _():
        from_right[...] = jnp.zeros_like(from_right)

    turned = jnp.transpose(scale[...])
    for b in range(blocks):
        scales[pl.ds(b * size, size), :] = jnp.broadcast_to(turned[:, b : b + 1], (size, 128))

    def smooth(c):
        here = pl.ds(pl.multiple_of(c * group, group), group)
        there = pl.ds(pl.multiple_of(rows - (c + 1) * group, group), group)
        left = from_left[here, :]
        right = from_right[here, :]
        for span, first, second, k in ((here, left, right, 0), (there, right, left, 1)):
            beside = jnp.where(lane, first.astype(f32), second.astype(f32)).astype(bf16)
            total = jnp.dot(field[span, :], mid[...], preferred_element_type=f32)
            total = total + jnp.dot(beside, halo[k], preferred_element_type=f32)
            weight = scales[span, :]
            pool[span, :] = (total * jnp.concatenate([weight] * (width // 128), 1)).astype(bf16)

    def across(o):
        later = 1 - (site + o) // site_total
        return pltpu.make_async_remote_copy(
            src_ref=pool.at[pl.ds(pl.multiple_of(later * (rows - group), group), group)],
            dst_ref=pool.at[pl.ds(pl.multiple_of(rows + site * group, group), group)],
            send_sem=gsend.at[o - 1],
            recv_sem=grecv.at[o - 1],
            device_id={"site": lax.rem(site + o, site_total)},
            device_id_type=MESH,
        )

    receive(0)
    smooth(0)
    for o in range(1, site_total):
        across(o).start()
    for n in range(1, len(pieces)):
        receive(n)
        lax.fori_loop(pieces[n][0], pieces[n][1], lambda c, _: (smooth(c), 0)[1], 0)

    for n in range(len(pieces)):

        @pl.when(step < time_total - 1)
        def _():
            sideways(n, True).wait_send()

        @pl.when(step > 0)
        def _():
            sideways(n, False).wait_send()

    for o in range(1, site_total):
        for copy, into, base, length, sem in (
            (points(o), geo, owned, 8, precv),
            (across(o), pool, rows, group, grecv),
        ):
            copy.wait_send()
            origin = lax.rem(site + site_total - o, site_total)
            landing = into.at[pl.ds(pl.multiple_of(base + origin * length, 8), length)]
            pltpu.make_async_remote_copy(
                src_ref=landing,
                dst_ref=landing,
                send_sem=sem.at[o - 1],
                recv_sem=sem.at[o - 1],
                device_id={"site": origin},
                device_id_type=MESH,
            ).wait_recv()


def combine_kernel(names, counts, pool, geo, scale, out, acc, tiles, across, upward, scales):
    site = lax.axis_index("site")
    blocks = scale.shape[0]
    size = tiles.shape[0]
    slots = names.shape[0] // blocks
    width = out.shape[1]
    for ref, source in (
        (across, geo[pl.ds(0, blocks), :]),
        (upward, geo[pl.ds(blocks, blocks), :]),
        (scales, scale[...]),
    ):
        turned = jnp.transpose(source)
        for b in range(blocks):
            ref[pl.ds(b * size, size), :] = jnp.broadcast_to(turned[:, b : b + 1], (size, 128))

    def named(b, k):
        name = names[b * slots + k]
        owner = name // blocks
        within = name - owner * blocks
        window = jnp.where(owner > site, within, within - (blocks - CAP))
        near = owner == site
        place = jnp.where(near, within, blocks + owner * CAP + window)
        first = jnp.where(near, within, 2 * blocks + 8 * owner + window)
        second = jnp.where(near, blocks + within, 2 * blocks + 8 * owner + window + CAP)
        return place, first, second

    def pair(b, k):
        count = counts[b]
        other = 2 * k + 1
        live = other < count
        return named(b, 2 * k), named(b, jnp.where(live, other, 2 * k)), live

    def build(b, k):
        one, two, live = pair(b, k)
        for j, (slot, weight) in enumerate(((one, 1.0), (two, jnp.where(live, 1.0, 0.0)))):
            x = geo[pl.ds(slot[1], 1), :]
            y = geo[pl.ds(slot[2], 1), :]
            for r in range(0, size, 32):
                span = pl.ds(pl.multiple_of(b * size + r, 32), 32)
                dx = across[span, :] - x
                dy = upward[span, :] - y
                square = dx * dx + dy * dy
                d = square * lax.rsqrt(jnp.maximum(square, 1e-30))
                t = jnp.maximum(1.0 - d, 0.0)
                t = t * t
                value = jnp.exp2(d * (-15.0 * math.log2(math.e))) * (t * t)
                value = value * (d * (4.0 * weight) + weight)
                tiles[pl.ds(r, 32), pl.ds(j * size, size)] = value.astype(bf16)

    def multiply(b, k):
        one, two, _ = pair(b, k)
        values = jnp.concatenate(
            [pool[pl.ds(pl.multiple_of(s[0] * size, size), size), :] for s in (one, two)]
        )
        product = jnp.dot(tiles[...], values, preferred_element_type=f32)
        total = jnp.where(k > 0, acc[...], 0.0) + product
        acc[...] = total
        return total

    def finish(b, total):
        span = pl.ds(pl.multiple_of(b * size, size), size)
        weight = jnp.concatenate([scales[span, :]] * (width // 128), 1)
        out[span, :] = (total * weight).astype(bf16)

    def pairs(b):
        return (counts[b] + 1) // 2

    build(0, 0)

    def block(b, _):
        def inner(k, _):
            multiply(b, k - 1)
            build(b, k)
            return 0

        last = pairs(b)
        lax.fori_loop(1, last, inner, 0)
        finish(b, multiply(b, last - 1))
        build(jnp.minimum(b + 1, blocks - 1), 0)
        return 0

    lax.fori_loop(0, blocks, block, 0)


def shards(
    site_total, time_total,
    site_field, positions, site_scale, neighbor_blocks, neighbor_count, lag_values, time_band,
):
    rows, width = site_field.shape
    blocks, slots = neighbor_blocks.shape
    size = rows // blocks
    reach = lag_values.shape[0] - 1
    group = CAP * size
    places = (positions.astype(f32) * (1.0 / 3.0)).reshape(2 * blocks, size)
    scale = site_scale.astype(f32).reshape(blocks, size)
    series = jnp.concatenate(
        [
            lag_values[reach:],
            jnp.zeros((2 * width - 2 * reach - 1,), f32),
            lag_values[:0:-1],
            lag_values[:reach],
        ]
    ).reshape(1, 2 * width)
    start = lax.axis_index("tm") * width
    padded = jnp.pad(time_band.astype(f32), (reach, reach))
    around = lax.dynamic_slice_in_dim(padded, start, width + 2 * reach)
    total = width + 2 * reach
    band = jnp.concatenate(
        [around, around[reach : reach + width], jnp.zeros((8 * 128 - total - width,), f32)]
    ).reshape(8, 128)
    vmem = pl.BlockSpec(memory_space=pltpu.VMEM)
    smem = pl.BlockSpec(memory_space=pltpu.SMEM)
    mid, halo = pl.pallas_call(
        table_kernel,
        out_shape=[
            jax.ShapeDtypeStruct((width, width), bf16),
            jax.ShapeDtypeStruct((2, 2 * reach, width), bf16),
        ],
        in_specs=[vmem] * 2,
        out_specs=[vmem] * 2,
        name="table",
    )(series, band)
    pool, geo = pl.pallas_call(
        functools.partial(exchange_kernel, site_total, time_total),
        out_shape=[
            jax.ShapeDtypeStruct((rows + site_total * group, width), bf16),
            jax.ShapeDtypeStruct((2 * blocks + 8 * site_total, size), f32),
        ],
        in_specs=[vmem] * 5,
        out_specs=[vmem] * 2,
        scratch_shapes=[
            pltpu.VMEM((rows // 2, 128), bf16),
            pltpu.VMEM((rows // 2, 128), bf16),
            pltpu.VMEM((rows // 2, 128), bf16),
            pltpu.VMEM((rows // 2, 128), bf16),
            pltpu.VMEM((rows, 128), f32),
            pltpu.VMEM((2, 8, 128), f32),
            pltpu.SemaphoreType.DMA((2, 3)),
            pltpu.SemaphoreType.DMA((2, 3)),
            pltpu.SemaphoreType.DMA((site_total - 1,)),
            pltpu.SemaphoreType.DMA((site_total - 1,)),
            pltpu.SemaphoreType.DMA((site_total - 1,)),
            pltpu.SemaphoreType.DMA((site_total - 1,)),
        ],
        compiler_params=pltpu.CompilerParams(
            collective_id=0, has_side_effects=True, vmem_limit_bytes=24 * 2**20
        ),
        name="exchange",
    )(site_field, mid, halo, places, scale)
    return pl.pallas_call(
        combine_kernel,
        out_shape=jax.ShapeDtypeStruct((rows, width), bf16),
        in_specs=[smem] * 2 + [vmem] * 3,
        out_specs=vmem,
        scratch_shapes=[
            pltpu.VMEM((size, width), f32),
            pltpu.VMEM((size, 2 * size), bf16),
            pltpu.VMEM((rows, 128), f32),
            pltpu.VMEM((rows, 128), f32),
            pltpu.VMEM((rows, 128), f32),
        ],
        compiler_params=pltpu.CompilerParams(vmem_limit_bytes=28 * 2**20),
        name="combine",
    )(neighbor_blocks.reshape(-1), neighbor_count, pool, geo, scale)


def solution(mesh):
    placed = (P("site", "tm"), P(None, "site"), P("site"), P("site", None), P("site"), P(), P())
    return jax.shard_map(
        functools.partial(shards, mesh.shape["site"], mesh.shape["tm"]),
        mesh=mesh,
        in_specs=placed,
        out_specs=P("site", "tm"),
        check_vma=False,
    )
```

```python
import functools
import math

import jax
import jax.numpy as jnp
from jax import lax
from jax.experimental import pallas as pl
from jax.experimental.pallas import tpu as pltpu
from jax.sharding import PartitionSpec as P

CAP = 2
MESH = pl.DeviceIdType.MESH
f32 = jnp.float32
bf16 = jnp.bfloat16


def table_kernel(lag_ref, band_ref, mid_ref, halo_ref, lags):
    step = lax.axis_index("tm")
    width = mid_ref.shape[0]
    reach = halo_ref.shape[1] // 2
    own = width // 128
    total = width + 256
    lags[...] = jnp.zeros_like(lags)
    lags[pl.ds(0, 1), pl.ds(0, reach + 1)] = lag_ref[...]
    lag_column = jnp.transpose(lags[...])[:, :1]
    lanes = 2 * width
    apart = jnp.abs(lax.broadcasted_iota(jnp.int32, (128, lanes), 1) - (lanes - 128))
    chosen = apart == lax.broadcasted_iota(jnp.int32, (128, lanes), 0)
    series = jnp.sum(
        jnp.where(chosen, jnp.broadcast_to(lag_column, (128, lanes)), 0.0), axis=0, keepdims=True
    )
    values = pltpu.roll(
        jnp.broadcast_to(series, (total, lanes)), 0, 1, stride=1, stride_axis=0
    )[:, :width]
    most = band_ref.shape[0] - 1
    before = band_ref[pl.ds(jnp.maximum(step * own - 1, 0), 1), :].astype(f32)
    after = band_ref[pl.ds(jnp.minimum(step * own + own, most), 1), :].astype(f32)
    here = [band_ref[pl.ds(step * own + j, 1), :].astype(f32) for j in range(own)]
    before = jnp.where(step > 0, before, 0.0)
    after = jnp.where(step * own + own <= most, after, 0.0)
    gathered = jnp.concatenate([before] + here + [after] + [before] * (8 - own - 2))
    turned = jnp.transpose(gathered)
    columns = jnp.concatenate(
        [jnp.broadcast_to(turned[:, j : j + 1], (128, width)) for j in range(own + 2)]
    )
    row = jnp.concatenate(here, 1)
    lag = jnp.abs(
        lax.broadcasted_iota(jnp.int32, (total, width), 0)
        - 128
        - lax.broadcasted_iota(jnp.int32, (total, width), 1)
    ).astype(f32)
    table = jnp.where(lag <= jnp.minimum(columns, row), values, 0.0).astype(bf16)
    first, last = table[128 - reach : 128], table[128 + width : 128 + width + reach]
    mid_ref[...] = table[128 : 128 + width]
    halo_ref[0] = jnp.concatenate([first, last])
    halo_ref[1] = jnp.concatenate([last, first])


def exchange_kernel(
    site_total, time_total, field_in, mid, halo, positions, scale, pool, geo, field, load,
    to_right, to_left, from_left, from_right, scales, edges,
    zsend, zrecv, gsend, grecv, psend, precv,
):
    site, step = lax.axis_index("site"), lax.axis_index("tm")
    rows, width = field.shape
    blocks = scale.shape[0]
    size = rows // blocks
    group = CAP * size
    chunks = rows // (2 * group)
    reach = width // 4
    owned = 2 * blocks

    fetch = pltpu.make_async_copy(field_in, field, load)
    fetch.start()
    barrier = pltpu.get_barrier_semaphore()
    for o in range(1, site_total):
        pl.semaphore_signal(
            barrier, inc=1, device_id={"site": lax.rem(site + o, site_total)}, device_id_type=MESH
        )

    for shift in (1, time_total - 1):
        pl.semaphore_signal(
            barrier, inc=1, device_id={"tm": lax.rem(step + shift, time_total)}, device_id_type=MESH
        )

    lane = lax.broadcasted_iota(jnp.int32, (group, 128), 1) < reach

    def pack(c):
        here = pl.ds(pl.multiple_of(c * group, group), group)
        there = pl.ds(pl.multiple_of(rows - (c + 1) * group, group), group)
        right_a = field[here, pl.ds(width - 128, 128)].astype(f32)
        right_b = field[there, pl.ds(width - 128, 128)].astype(f32)
        left_a = field[here, pl.ds(0, 128)].astype(f32)
        left_b = field[there, pl.ds(0, 128)].astype(f32)
        to_right[here, :] = jnp.where(lane, pltpu.roll(right_a, 64, 1), right_b).astype(bf16)
        to_left[here, :] = jnp.where(lane, left_b, pltpu.roll(left_a, 64, 1)).astype(bf16)

    for j in range(2):
        line = positions[pl.ds(j, 1), :].astype(f32) * (1.0 / 3.0)
        for b in range(blocks):
            geo[pl.ds(j * blocks + b, 1), :] = line[:, b * size : (b + 1) * size]
    turned = jnp.transpose(scale[...])
    for b in range(blocks):
        scales[pl.ds(b * size, size), :] = jnp.broadcast_to(turned[:, b : b + 1], (size, 128))
    fetch.wait()
    pack(0)
    for k in range(2):
        start = k * (blocks - CAP)
        for j in range(2):
            edges[k, pl.ds(j * CAP, CAP), :] = geo[pl.ds(j * blocks + start, CAP), :]
        edges[k, pl.ds(2 * CAP, 8 - 2 * CAP), :] = jnp.zeros((8 - 2 * CAP, 128), f32)

    pl.semaphore_wait(barrier, site_total + 1)

    pieces = [(0, 1), (1, chunks // 2), (chunks // 2, chunks)]

    def sideways(n, right):
        first, last = pieces[n]
        span = pl.ds(first * group, (last - first) * group)
        way = 0 if right else 1
        return pltpu.make_async_remote_copy(
            src_ref=(to_right if right else to_left).at[span],
            dst_ref=(from_left if right else from_right).at[span],
            send_sem=zsend.at[way, n],
            recv_sem=zrecv.at[way, n],
            device_id={"tm": (step + 1) if right else (step - 1)},
            device_id_type=MESH,
        )

    def send(n):
        @pl.when(step < time_total - 1)
        def _():
            sideways(n, True).start()

        @pl.when(step > 0)
        def _():
            sideways(n, False).start()

    def receive(n):
        @pl.when(step > 0)
        def _():
            sideways(n, True).wait_recv()

        @pl.when(step < time_total - 1)
        def _():
            sideways(n, False).wait_recv()

    send(0)

    def points(o):
        later = 1 - (site + o) // site_total
        return pltpu.make_async_remote_copy(
            src_ref=edges.at[later],
            dst_ref=geo.at[pl.ds(owned + 8 * site, 8)],
            send_sem=psend.at[o - 1],
            recv_sem=precv.at[o - 1],
            device_id={"site": lax.rem(site + o, site_total)},
            device_id_type=MESH,
        )

    for o in range(1, site_total):
        points(o).start()

    for n in range(1, len(pieces)):
        lax.fori_loop(pieces[n][0], pieces[n][1], lambda c, _: (pack(c), 0)[1], 0)
        send(n)

    @pl.when(step == 0)
    def _():
        from_left[...] = jnp.zeros_like(from_left)

    @pl.when(step == time_total - 1)
    def _():
        from_right[...] = jnp.zeros_like(from_right)

    def smooth(c):
        here = pl.ds(pl.multiple_of(c * group, group), group)
        there = pl.ds(pl.multiple_of(rows - (c + 1) * group, group), group)
        left = from_left[here, :]
        right = from_right[here, :]
        for span, first, second, k in ((here, left, right, 0), (there, right, left, 1)):
            beside = jnp.where(lane, first.astype(f32), second.astype(f32)).astype(bf16)
            total = jnp.dot(field[span, :], mid[...], preferred_element_type=f32)
            total = total + jnp.dot(beside, halo[k], preferred_element_type=f32)
            weight = scales[span, :]
            pool[span, :] = (total * jnp.concatenate([weight] * (width // 128), 1)).astype(bf16)

    def across(o):
        later = 1 - (site + o) // site_total
        return pltpu.make_async_remote_copy(
            src_ref=pool.at[pl.ds(pl.multiple_of(later * (rows - group), group), group)],
            dst_ref=pool.at[pl.ds(pl.multiple_of(rows + site * group, group), group)],
            send_sem=gsend.at[o - 1],
            recv_sem=grecv.at[o - 1],
            device_id={"site": lax.rem(site + o, site_total)},
            device_id_type=MESH,
        )

    receive(0)
    smooth(0)
    for o in range(1, site_total):
        across(o).start()
    for n in range(1, len(pieces)):
        receive(n)
        lax.fori_loop(pieces[n][0], pieces[n][1], lambda c, _: (smooth(c), 0)[1], 0)

    for n in range(len(pieces)):

        @pl.when(step < time_total - 1)
        def _():
            sideways(n, True).wait_send()

        @pl.when(step > 0)
        def _():
            sideways(n, False).wait_send()

    for o in range(1, site_total):
        for copy, into, base, length, sem in (
            (points(o), geo, owned, 8, precv),
            (across(o), pool, rows, group, grecv),
        ):
            copy.wait_send()
            origin = lax.rem(site + site_total - o, site_total)
            landing = into.at[pl.ds(pl.multiple_of(base + origin * length, 8), length)]
            pltpu.make_async_remote_copy(
                src_ref=landing,
                dst_ref=landing,
                send_sem=sem.at[o - 1],
                recv_sem=sem.at[o - 1],
                device_id={"site": origin},
                device_id_type=MESH,
            ).wait_recv()


def combine_kernel(names, counts, pool, geo, scale, out, acc, tiles, across, upward, scales):
    site = lax.axis_index("site")
    blocks = scale.shape[0]
    size = tiles.shape[0]
    lanes = tiles.shape[1] // size
    width = out.shape[1]
    for ref, source in (
        (across, geo[pl.ds(0, blocks), :]),
        (upward, geo[pl.ds(blocks, blocks), :]),
        (scales, scale[...]),
    ):
        turned = jnp.transpose(source)
        for b in range(blocks):
            ref[pl.ds(b * size, size), :] = jnp.broadcast_to(turned[:, b : b + 1], (size, 128))

    def named(b, k):
        name = names[b, k]
        owner = name // blocks
        within = name - owner * blocks
        window = jnp.where(owner > site, within, within - (blocks - CAP))
        near = owner == site
        place = jnp.where(near, within, blocks + owner * CAP + window)
        first = jnp.where(near, within, 2 * blocks + 8 * owner + window)
        second = jnp.where(near, blocks + within, 2 * blocks + 8 * owner + window + CAP)
        return place, first, second

    def several(b, k):
        last = counts[b] - 1
        found = []
        for j in range(lanes):
            n = lanes * k + j
            found.append((named(b, jnp.minimum(n, last)), jnp.where(n <= last, 1.0, 0.0)))
        return found

    def build(b, k):
        for j, (slot, weight) in enumerate(several(b, k)):
            x = geo[pl.ds(slot[1], 1), :]
            y = geo[pl.ds(slot[2], 1), :]
            for r in range(0, size, 32):
                span = pl.ds(pl.multiple_of(b * size + r, 32), 32)
                dx = across[span, :] - x
                dy = upward[span, :] - y
                square = dx * dx + dy * dy
                d = square * lax.rsqrt(jnp.maximum(square, 1e-30))
                t = jnp.maximum(1.0 - d, 0.0)
                t = t * t
                value = jnp.exp2(d * (-15.0 * math.log2(math.e))) * (t * t)
                value = value * (d * (4.0 * weight) + weight)
                tiles[pl.ds(r, 32), pl.ds(j * size, size)] = value.astype(bf16)

    def multiply(b, k):
        values = jnp.concatenate(
            [pool[pl.ds(pl.multiple_of(s[0] * size, size), size), :] for s, _ in several(b, k)]
        )
        product = jnp.dot(tiles[...], values, preferred_element_type=f32)
        total = jnp.where(k > 0, acc[...], 0.0) + product
        acc[...] = total
        return total

    def finish(b, total):
        span = pl.ds(pl.multiple_of(b * size, size), size)
        weight = jnp.concatenate([scales[span, :]] * (width // 128), 1)
        out[span, :] = (total * weight).astype(bf16)

    def turns(b):
        return (counts[b] + lanes - 1) // lanes

    build(0, 0)

    def block(b, _):
        def inner(k, _):
            multiply(b, k - 1)
            build(b, k)
            return 0

        last = turns(b)
        lax.fori_loop(1, last, inner, 0)
        finish(b, multiply(b, last - 1))
        build(jnp.minimum(b + 1, blocks - 1), 0)
        return 0

    lax.fori_loop(0, blocks, block, 0)


def shards(
    site_total, time_total,
    site_field, positions, site_scale, neighbor_blocks, neighbor_count, lag_values, time_band,
):
    rows, width = site_field.shape
    blocks = neighbor_count.shape[0]
    size = rows // blocks
    reach = lag_values.shape[0] - 1
    group = CAP * size
    scale = site_scale.astype(f32).reshape(blocks, size)
    vmem = pl.BlockSpec(memory_space=pltpu.VMEM)
    smem = pl.BlockSpec(memory_space=pltpu.SMEM)
    mid, halo = pl.pallas_call(
        table_kernel,
        out_shape=[
            jax.ShapeDtypeStruct((width, width), bf16),
            jax.ShapeDtypeStruct((2, 2 * reach, width), bf16),
        ],
        in_specs=[vmem] * 2,
        out_specs=[vmem] * 2,
        scratch_shapes=[pltpu.VMEM((8, 128), f32)],
        compiler_params=pltpu.CompilerParams(vmem_limit_bytes=12 * 2**20),
        name="table",
    )(lag_values.reshape(1, -1), time_band.reshape(-1, 128))
    pool, geo = pl.pallas_call(
        functools.partial(exchange_kernel, site_total, time_total),
        out_shape=[
            jax.ShapeDtypeStruct((rows + site_total * group, width), bf16),
            jax.ShapeDtypeStruct((2 * blocks + 8 * site_total, size), f32),
        ],
        in_specs=[pl.BlockSpec(memory_space=pltpu.HBM)] + [vmem] * 4,
        out_specs=[vmem] * 2,
        scratch_shapes=[
            pltpu.VMEM((rows, width), bf16),
            pltpu.SemaphoreType.DMA,
            pltpu.VMEM((rows // 2, 128), bf16),
            pltpu.VMEM((rows // 2, 128), bf16),
            pltpu.VMEM((rows // 2, 128), bf16),
            pltpu.VMEM((rows // 2, 128), bf16),
            pltpu.VMEM((rows, 128), f32),
            pltpu.VMEM((2, 8, 128), f32),
            pltpu.SemaphoreType.DMA((2, 3)),
            pltpu.SemaphoreType.DMA((2, 3)),
            pltpu.SemaphoreType.DMA((site_total - 1,)),
            pltpu.SemaphoreType.DMA((site_total - 1,)),
            pltpu.SemaphoreType.DMA((site_total - 1,)),
            pltpu.SemaphoreType.DMA((site_total - 1,)),
        ],
        compiler_params=pltpu.CompilerParams(
            collective_id=0, has_side_effects=True, vmem_limit_bytes=24 * 2**20
        ),
        name="exchange",
    )(site_field, mid, halo, positions, scale)
    return pl.pallas_call(
        combine_kernel,
        out_shape=jax.ShapeDtypeStruct((rows, width), bf16),
        in_specs=[smem] * 2 + [vmem] * 3,
        out_specs=vmem,
        scratch_shapes=[
            pltpu.VMEM((size, width), f32),
            pltpu.VMEM((size, 4 * size), bf16),
            pltpu.VMEM((rows, 128), f32),
            pltpu.VMEM((rows, 128), f32),
            pltpu.VMEM((rows, 128), f32),
        ],
        compiler_params=pltpu.CompilerParams(vmem_limit_bytes=28 * 2**20),
        name="combine",
    )(neighbor_blocks, neighbor_count, pool, geo, scale)


def solution(mesh):
    placed = (P("site", "tm"), P(None, "site"), P("site"), P("site", None), P("site"), P(), P())
    return jax.shard_map(
        functools.partial(shards, mesh.shape["site"], mesh.shape["tm"]),
        mesh=mesh,
        in_specs=placed,
        out_specs=P("site", "tm"),
        check_vma=False,
    )
```

```python
import functools
import math

import jax
import jax.numpy as jnp
from jax import lax
from jax.experimental import pallas as pl
from jax.experimental.pallas import tpu as pltpu
from jax.sharding import PartitionSpec as P

CAP = 2
LANES = 4
MESH = pl.DeviceIdType.MESH
f32 = jnp.float32
bf16 = jnp.bfloat16


def table_kernel(lag_ref, band_ref, mid_ref, halo_ref, lags):
    step = lax.axis_index("tm")
    width = mid_ref.shape[0]
    reach = halo_ref.shape[1] // 2
    own = width // 128
    total = width + 256
    lags[...] = jnp.zeros_like(lags)
    lags[pl.ds(0, 1), pl.ds(0, reach + 1)] = lag_ref[...]
    lag_column = jnp.transpose(lags[...])[:, :1]
    lanes = 2 * width
    apart = jnp.abs(lax.broadcasted_iota(jnp.int32, (128, lanes), 1) - (lanes - 128))
    chosen = apart == lax.broadcasted_iota(jnp.int32, (128, lanes), 0)
    series = jnp.sum(
        jnp.where(chosen, jnp.broadcast_to(lag_column, (128, lanes)), 0.0), axis=0, keepdims=True
    )
    values = pltpu.roll(
        jnp.broadcast_to(series, (total, lanes)), 0, 1, stride=1, stride_axis=0
    )[:, :width]
    most = band_ref.shape[0] - 1
    before = band_ref[pl.ds(jnp.maximum(step * own - 1, 0), 1), :].astype(f32)
    after = band_ref[pl.ds(jnp.minimum(step * own + own, most), 1), :].astype(f32)
    here = [band_ref[pl.ds(step * own + j, 1), :].astype(f32) for j in range(own)]
    before = jnp.where(step > 0, before, 0.0)
    after = jnp.where(step * own + own <= most, after, 0.0)
    gathered = jnp.concatenate([before] + here + [after] + [before] * (8 - own - 2))
    turned = jnp.transpose(gathered)
    columns = jnp.concatenate(
        [jnp.broadcast_to(turned[:, j : j + 1], (128, width)) for j in range(own + 2)]
    )
    row = jnp.concatenate(here, 1)
    lag = jnp.abs(
        lax.broadcasted_iota(jnp.int32, (total, width), 0)
        - 128
        - lax.broadcasted_iota(jnp.int32, (total, width), 1)
    ).astype(f32)
    table = jnp.where(lag <= jnp.minimum(columns, row), values, 0.0).astype(bf16)
    first, last = table[128 - reach : 128], table[128 + width : 128 + width + reach]
    mid_ref[...] = table[128 : 128 + width]
    halo_ref[0] = jnp.concatenate([first, last])
    halo_ref[1] = jnp.concatenate([last, first])


def several(names, counts, site, b, k, blocks):
    last = jnp.maximum(counts[b] - 1, 0)
    found = []
    for j in range(LANES):
        n = LANES * k + j
        name = names[b, jnp.minimum(n, last)]
        owner = name // blocks
        within = name - owner * blocks
        window = jnp.where(owner > site, within, within - (blocks - CAP))
        window = jnp.clip(window, 0, CAP - 1)
        near = owner == site
        place = jnp.where(near, within, blocks + owner * CAP + window)
        first = jnp.where(near, within, 2 * blocks + 8 * owner + window)
        second = jnp.where(near, blocks + within, 2 * blocks + 8 * owner + window + CAP)
        found.append((place, first, second, jnp.where(n <= last, 1.0, 0.0)))
    return found


def build_tiles(found, b, geo, across, upward, tiles):
    size = tiles.shape[0]
    for j, (_, first, second, weight) in enumerate(found):
        x = geo[pl.ds(first, 1), :]
        y = geo[pl.ds(second, 1), :]
        for r in range(0, size, 32):
            span = pl.ds(pl.multiple_of(b * size + r, 32), 32)
            dx = across[span, :] - x
            dy = upward[span, :] - y
            square = dx * dx + dy * dy
            d = square * lax.rsqrt(jnp.maximum(square, 1e-30))
            t = jnp.maximum(1.0 - d, 0.0)
            t = t * t
            value = jnp.exp2(d * (-15.0 * math.log2(math.e))) * (t * t)
            value = value * (d * (4.0 * weight) + weight)
            tiles[pl.ds(r, 32), pl.ds(j * size, size)] = value.astype(bf16)


def exchange_kernel(
    site_total, time_total, field_in, mid, halo, positions, scale, names, counts,
    pool, geo, ready, across_rows, upward_rows, field, load,
    to_right, to_left, from_left, from_right, scales, edges,
    zsend, zrecv, gsend, grecv, psend, precv,
):
    site, step = lax.axis_index("site"), lax.axis_index("tm")
    rows, width = field.shape
    blocks = scale.shape[0]
    size = rows // blocks
    group = CAP * size
    chunks = rows // (2 * group)
    reach = width // 4
    owned = 2 * blocks

    fetch = pltpu.make_async_copy(field_in, field, load)
    fetch.start()
    barrier = pltpu.get_barrier_semaphore()
    for o in range(1, site_total):
        pl.semaphore_signal(
            barrier, inc=1, device_id={"site": lax.rem(site + o, site_total)}, device_id_type=MESH
        )

    for shift in (1, time_total - 1):
        pl.semaphore_signal(
            barrier, inc=1, device_id={"tm": lax.rem(step + shift, time_total)}, device_id_type=MESH
        )

    lane = lax.broadcasted_iota(jnp.int32, (group, 128), 1) < reach

    def pack(c):
        here = pl.ds(pl.multiple_of(c * group, group), group)
        there = pl.ds(pl.multiple_of(rows - (c + 1) * group, group), group)
        right_a = field[here, pl.ds(width - 128, 128)].astype(f32)
        right_b = field[there, pl.ds(width - 128, 128)].astype(f32)
        left_a = field[here, pl.ds(0, 128)].astype(f32)
        left_b = field[there, pl.ds(0, 128)].astype(f32)
        to_right[here, :] = jnp.where(lane, pltpu.roll(right_a, 64, 1), right_b).astype(bf16)
        to_left[here, :] = jnp.where(lane, left_b, pltpu.roll(left_a, 64, 1)).astype(bf16)

    for j in range(2):
        line = positions[pl.ds(j, 1), :].astype(f32) * (1.0 / 3.0)
        for b in range(blocks):
            geo[pl.ds(j * blocks + b, 1), :] = line[:, b * size : (b + 1) * size]
    turned = jnp.transpose(scale[...])
    for b in range(blocks):
        scales[pl.ds(b * size, size), :] = jnp.broadcast_to(turned[:, b : b + 1], (size, 128))
    fetch.wait()
    pack(0)
    for k in range(2):
        start = k * (blocks - CAP)
        for j in range(2):
            edges[k, pl.ds(j * CAP, CAP), :] = geo[pl.ds(j * blocks + start, CAP), :]
        edges[k, pl.ds(2 * CAP, 8 - 2 * CAP), :] = jnp.zeros((8 - 2 * CAP, 128), f32)
    geo[pl.ds(pl.multiple_of(owned + 8 * site, 8), 8), :] = jnp.zeros((8, 128), f32)

    pl.semaphore_wait(barrier, site_total + 1)

    pieces = [(0, 1), (1, chunks // 2), (chunks // 2, chunks)]

    def sideways(n, right):
        first, last = pieces[n]
        span = pl.ds(first * group, (last - first) * group)
        way = 0 if right else 1
        return pltpu.make_async_remote_copy(
            src_ref=(to_right if right else to_left).at[span],
            dst_ref=(from_left if right else from_right).at[span],
            send_sem=zsend.at[way, n],
            recv_sem=zrecv.at[way, n],
            device_id={"tm": (step + 1) if right else (step - 1)},
            device_id_type=MESH,
        )

    def send(n):
        @pl.when(step < time_total - 1)
        def _():
            sideways(n, True).start()

        @pl.when(step > 0)
        def _():
            sideways(n, False).start()

    def receive(n):
        @pl.when(step > 0)
        def _():
            sideways(n, True).wait_recv()

        @pl.when(step < time_total - 1)
        def _():
            sideways(n, False).wait_recv()

    send(0)

    def points(o):
        later = 1 - (site + o) // site_total
        return pltpu.make_async_remote_copy(
            src_ref=edges.at[later],
            dst_ref=geo.at[pl.ds(owned + 8 * site, 8)],
            send_sem=psend.at[o - 1],
            recv_sem=precv.at[o - 1],
            device_id={"site": lax.rem(site + o, site_total)},
            device_id_type=MESH,
        )

    for o in range(1, site_total):
        points(o).start()

    for n in range(1, len(pieces)):
        lax.fori_loop(pieces[n][0], pieces[n][1], lambda c, _: (pack(c), 0)[1], 0)
        send(n)

    @pl.when(step == 0)
    def _():
        from_left[...] = jnp.zeros_like(from_left)

    @pl.when(step == time_total - 1)
    def _():
        from_right[...] = jnp.zeros_like(from_right)

    for ref, base in ((across_rows, 0), (upward_rows, blocks)):
        turned = jnp.transpose(geo[pl.ds(base, blocks), :])
        for b in range(blocks):
            ref[pl.ds(b * size, size), :] = jnp.broadcast_to(turned[:, b : b + 1], (size, 128))

    def smooth(c):
        here = pl.ds(pl.multiple_of(c * group, group), group)
        there = pl.ds(pl.multiple_of(rows - (c + 1) * group, group), group)
        left = from_left[here, :]
        right = from_right[here, :]
        for span, first, second, k in ((here, left, right, 0), (there, right, left, 1)):
            beside = jnp.where(lane, first.astype(f32), second.astype(f32)).astype(bf16)
            total = jnp.dot(field[span, :], mid[...], preferred_element_type=f32)
            total = total + jnp.dot(beside, halo[k], preferred_element_type=f32)
            weight = scales[span, :]
            pool[span, :] = (total * jnp.concatenate([weight] * (width // 128), 1)).astype(bf16)

    def across(o):
        later = 1 - (site + o) // site_total
        return pltpu.make_async_remote_copy(
            src_ref=pool.at[pl.ds(pl.multiple_of(later * (rows - group), group), group)],
            dst_ref=pool.at[pl.ds(pl.multiple_of(rows + site * group, group), group)],
            send_sem=gsend.at[o - 1],
            recv_sem=grecv.at[o - 1],
            device_id={"site": lax.rem(site + o, site_total)},
            device_id_type=MESH,
        )

    receive(0)
    smooth(0)
    for o in range(1, site_total):
        across(o).start()

    def landed(o, into, base, length, sem):
        origin = lax.rem(site + site_total - o, site_total)
        landing = into.at[pl.ds(pl.multiple_of(base + origin * length, 8), length)]
        pltpu.make_async_remote_copy(
            src_ref=landing,
            dst_ref=landing,
            send_sem=sem.at[o - 1],
            recv_sem=sem.at[o - 1],
            device_id={"site": origin},
            device_id_type=MESH,
        ).wait_recv()

    for o in range(1, site_total):
        points(o).wait_send()
        landed(o, geo, owned, 8, precv)

    def prepare(b, _):
        found = several(names, counts, site, b, 0, blocks)
        build_tiles(found, b, geo, across_rows, upward_rows, ready.at[b])
        return 0

    lax.fori_loop(0, blocks, prepare, 0)
    for n in range(1, len(pieces)):
        receive(n)
        lax.fori_loop(pieces[n][0], pieces[n][1], lambda c, _: (smooth(c), 0)[1], 0)

    for n in range(len(pieces)):

        @pl.when(step < time_total - 1)
        def _():
            sideways(n, True).wait_send()

        @pl.when(step > 0)
        def _():
            sideways(n, False).wait_send()

    for o in range(1, site_total):
        across(o).wait_send()
        landed(o, pool, rows, group, grecv)


def combine_kernel(names, counts, pool, geo, ready, scale, out, acc, tiles, across, upward, scales):
    site = lax.axis_index("site")
    blocks = scale.shape[0]
    size = tiles.shape[0]
    width = out.shape[1]
    for ref, source in (
        (across, geo[pl.ds(0, blocks), :]),
        (upward, geo[pl.ds(blocks, blocks), :]),
        (scales, scale[...]),
    ):
        turned = jnp.transpose(source)
        for b in range(blocks):
            ref[pl.ds(b * size, size), :] = jnp.broadcast_to(turned[:, b : b + 1], (size, 128))

    def build(b, k):
        found = several(names, counts, site, b, k, blocks)
        build_tiles(found, b, geo, across, upward, tiles)

    def values(b, k):
        found = several(names, counts, site, b, k, blocks)
        return jnp.concatenate(
            [pool[pl.ds(pl.multiple_of(s[0] * size, size), size), :] for s in found]
        )

    def multiply(b, k):
        product = jnp.dot(tiles[...], values(b, k), preferred_element_type=f32)
        total = jnp.where(k > 1, acc[...], 0.0) + product
        acc[...] = total
        return total

    def finish(b, total):
        total = total + jnp.dot(ready[b], values(b, 0), preferred_element_type=f32)
        span = pl.ds(pl.multiple_of(b * size, size), size)
        weight = jnp.concatenate([scales[span, :]] * (width // 128), 1)
        out[span, :] = (total * weight).astype(bf16)

    def turns(b):
        return jnp.maximum((counts[b] + LANES - 1) // LANES, 2)

    build(0, 1)

    def block(b, _):
        def inner(k, _):
            multiply(b, k - 1)
            build(b, k)
            return 0

        last = turns(b)
        lax.fori_loop(2, last, inner, 0)
        finish(b, multiply(b, last - 1))
        build(jnp.minimum(b + 1, blocks - 1), 1)
        return 0

    lax.fori_loop(0, blocks, block, 0)


def shards(
    site_total, time_total,
    site_field, positions, site_scale, neighbor_blocks, neighbor_count, lag_values, time_band,
):
    rows, width = site_field.shape
    blocks = neighbor_count.shape[0]
    size = rows // blocks
    reach = lag_values.shape[0] - 1
    group = CAP * size
    scale = site_scale.astype(f32).reshape(blocks, size)
    vmem = pl.BlockSpec(memory_space=pltpu.VMEM)
    smem = pl.BlockSpec(memory_space=pltpu.SMEM)
    mid, halo = pl.pallas_call(
        table_kernel,
        out_shape=[
            jax.ShapeDtypeStruct((width, width), bf16),
            jax.ShapeDtypeStruct((2, 2 * reach, width), bf16),
        ],
        in_specs=[vmem] * 2,
        out_specs=[vmem] * 2,
        scratch_shapes=[pltpu.VMEM((8, 128), f32)],
        compiler_params=pltpu.CompilerParams(vmem_limit_bytes=12 * 2**20),
        name="table",
    )(lag_values.reshape(1, -1), time_band.reshape(-1, 128))
    pool, geo, ready = pl.pallas_call(
        functools.partial(exchange_kernel, site_total, time_total),
        out_shape=[
            jax.ShapeDtypeStruct((rows + site_total * group, width), bf16),
            jax.ShapeDtypeStruct((2 * blocks + 8 * site_total, size), f32),
            jax.ShapeDtypeStruct((blocks, size, LANES * size), bf16),
        ],
        in_specs=[pl.BlockSpec(memory_space=pltpu.HBM)] + [vmem] * 4 + [smem] * 2,
        out_specs=[vmem] * 3,
        scratch_shapes=[
            pltpu.VMEM((rows, 128), f32),
            pltpu.VMEM((rows, 128), f32),
            pltpu.VMEM((rows, width), bf16),
            pltpu.SemaphoreType.DMA,
            pltpu.VMEM((rows // 2, 128), bf16),
            pltpu.VMEM((rows // 2, 128), bf16),
            pltpu.VMEM((rows // 2, 128), bf16),
            pltpu.VMEM((rows // 2, 128), bf16),
            pltpu.VMEM((rows, 128), f32),
            pltpu.VMEM((2, 8, 128), f32),
            pltpu.SemaphoreType.DMA((2, 3)),
            pltpu.SemaphoreType.DMA((2, 3)),
            pltpu.SemaphoreType.DMA((site_total - 1,)),
            pltpu.SemaphoreType.DMA((site_total - 1,)),
            pltpu.SemaphoreType.DMA((site_total - 1,)),
            pltpu.SemaphoreType.DMA((site_total - 1,)),
        ],
        compiler_params=pltpu.CompilerParams(
            collective_id=0, has_side_effects=True, vmem_limit_bytes=24 * 2**20
        ),
        name="exchange",
    )(site_field, mid, halo, positions, scale, neighbor_blocks, neighbor_count)
    return pl.pallas_call(
        combine_kernel,
        out_shape=jax.ShapeDtypeStruct((rows, width), bf16),
        in_specs=[smem] * 2 + [vmem] * 4,
        out_specs=vmem,
        scratch_shapes=[
            pltpu.VMEM((size, width), f32),
            pltpu.VMEM((size, LANES * size), bf16),
            pltpu.VMEM((rows, 128), f32),
            pltpu.VMEM((rows, 128), f32),
            pltpu.VMEM((rows, 128), f32),
        ],
        compiler_params=pltpu.CompilerParams(vmem_limit_bytes=28 * 2**20),
        name="combine",
    )(neighbor_blocks, neighbor_count, pool, geo, ready, scale)


def solution(mesh):
    placed = (P("site", "tm"), P(None, "site"), P("site"), P("site", None), P("site"), P(), P())
    return jax.shard_map(
        functools.partial(shards, mesh.shape["site"], mesh.shape["tm"]),
        mesh=mesh,
        in_specs=placed,
        out_specs=P("site", "tm"),
        check_vma=False,
    )
```

```python
import functools
import math

import jax
import jax.numpy as jnp
from jax import lax
from jax.experimental import pallas as pl
from jax.experimental.pallas import tpu as pltpu
from jax.sharding import PartitionSpec as P

CAP = 2
MESH = pl.DeviceIdType.MESH
f32 = jnp.float32
bf16 = jnp.bfloat16


def table_kernel(lag_ref, band_ref, mid_ref, halo_ref, lags):
    step = lax.axis_index("tm")
    width = mid_ref.shape[0]
    reach = halo_ref.shape[1] // 2
    own = width // 128
    total = width + 256
    lags[...] = jnp.zeros_like(lags)
    lags[pl.ds(0, 1), pl.ds(0, reach + 1)] = lag_ref[...]
    lag_column = jnp.transpose(lags[...])[:, :1]
    lanes = 2 * width
    apart = jnp.abs(lax.broadcasted_iota(jnp.int32, (128, lanes), 1) - (lanes - 128))
    chosen = apart == lax.broadcasted_iota(jnp.int32, (128, lanes), 0)
    series = jnp.sum(
        jnp.where(chosen, jnp.broadcast_to(lag_column, (128, lanes)), 0.0), axis=0, keepdims=True
    )
    values = pltpu.roll(
        jnp.broadcast_to(series, (total, lanes)), 0, 1, stride=1, stride_axis=0
    )[:, :width]
    most = band_ref.shape[0] - 1
    before = band_ref[pl.ds(jnp.maximum(step * own - 1, 0), 1), :].astype(f32)
    after = band_ref[pl.ds(jnp.minimum(step * own + own, most), 1), :].astype(f32)
    here = [band_ref[pl.ds(step * own + j, 1), :].astype(f32) for j in range(own)]
    before = jnp.where(step > 0, before, 0.0)
    after = jnp.where(step * own + own <= most, after, 0.0)
    gathered = jnp.concatenate([before] + here + [after] + [before] * (8 - own - 2))
    turned = jnp.transpose(gathered)
    columns = jnp.concatenate(
        [jnp.broadcast_to(turned[:, j : j + 1], (128, width)) for j in range(own + 2)]
    )
    row = jnp.concatenate(here, 1)
    lag = jnp.abs(
        lax.broadcasted_iota(jnp.int32, (total, width), 0)
        - 128
        - lax.broadcasted_iota(jnp.int32, (total, width), 1)
    ).astype(f32)
    table = jnp.where(lag <= jnp.minimum(columns, row), values, 0.0).astype(bf16)
    first, last = table[128 - reach : 128], table[128 + width : 128 + width + reach]
    mid_ref[...] = table[128 : 128 + width]
    halo_ref[0] = jnp.concatenate([first, last])
    halo_ref[1] = jnp.concatenate([last, first])


def exchange_kernel(
    site_total, time_total, field_in, mid, halo, positions, scale, pool, geo, field, load,
    to_right, to_left, from_left, from_right, scales, edges,
    zsend, zrecv, gsend, grecv, psend, precv,
):
    site, step = lax.axis_index("site"), lax.axis_index("tm")
    rows, width = field.shape
    blocks = scale.shape[0]
    size = rows // blocks
    group = CAP * size
    chunks = rows // (2 * group)
    reach = width // 4
    owned = 2 * blocks

    fetch = pltpu.make_async_copy(field_in, field, load)
    fetch.start()
    barrier = pltpu.get_barrier_semaphore()
    for o in range(1, site_total):
        pl.semaphore_signal(
            barrier, inc=1, device_id={"site": lax.rem(site + o, site_total)}, device_id_type=MESH
        )

    for shift in (1, time_total - 1):
        pl.semaphore_signal(
            barrier, inc=1, device_id={"tm": lax.rem(step + shift, time_total)}, device_id_type=MESH
        )

    lane = lax.broadcasted_iota(jnp.int32, (group, 128), 1) < reach

    def pack(c):
        here = pl.ds(pl.multiple_of(c * group, group), group)
        there = pl.ds(pl.multiple_of(rows - (c + 1) * group, group), group)
        right_a = field[here, pl.ds(width - 128, 128)].astype(f32)
        right_b = field[there, pl.ds(width - 128, 128)].astype(f32)
        left_a = field[here, pl.ds(0, 128)].astype(f32)
        left_b = field[there, pl.ds(0, 128)].astype(f32)
        to_right[here, :] = jnp.where(lane, pltpu.roll(right_a, 64, 1), right_b).astype(bf16)
        to_left[here, :] = jnp.where(lane, left_b, pltpu.roll(left_a, 64, 1)).astype(bf16)

    for j in range(2):
        line = positions[pl.ds(j, 1), :].astype(f32) * (1.0 / 3.0)
        for b in range(blocks):
            geo[pl.ds(j * blocks + b, 1), :] = line[:, b * size : (b + 1) * size]
    turned = jnp.transpose(scale[...])
    for b in range(blocks):
        scales[pl.ds(b * size, size), :] = jnp.broadcast_to(turned[:, b : b + 1], (size, 128))
    fetch.wait()
    pack(0)
    for k in range(2):
        start = k * (blocks - CAP)
        for j in range(2):
            edges[k, pl.ds(j * CAP, CAP), :] = geo[pl.ds(j * blocks + start, CAP), :]
        edges[k, pl.ds(2 * CAP, 8 - 2 * CAP), :] = jnp.zeros((8 - 2 * CAP, 128), f32)

    pl.semaphore_wait(barrier, site_total + 1)

    pieces = [(0, 1), (1, chunks // 2), (chunks // 2, chunks)]

    def sideways(n, right):
        first, last = pieces[n]
        span = pl.ds(first * group, (last - first) * group)
        way = 0 if right else 1
        return pltpu.make_async_remote_copy(
            src_ref=(to_right if right else to_left).at[span],
            dst_ref=(from_left if right else from_right).at[span],
            send_sem=zsend.at[way, n],
            recv_sem=zrecv.at[way, n],
            device_id={"tm": (step + 1) if right else (step - 1)},
            device_id_type=MESH,
        )

    def send(n):
        @pl.when(step < time_total - 1)
        def _():
            sideways(n, True).start()

        @pl.when(step > 0)
        def _():
            sideways(n, False).start()

    def receive(n):
        @pl.when(step > 0)
        def _():
            sideways(n, True).wait_recv()

        @pl.when(step < time_total - 1)
        def _():
            sideways(n, False).wait_recv()

    send(0)

    def points(o):
        later = 1 - (site + o) // site_total
        return pltpu.make_async_remote_copy(
            src_ref=edges.at[later],
            dst_ref=geo.at[pl.ds(owned + 8 * site, 8)],
            send_sem=psend.at[o - 1],
            recv_sem=precv.at[o - 1],
            device_id={"site": lax.rem(site + o, site_total)},
            device_id_type=MESH,
        )

    for o in range(1, site_total):
        points(o).start()

    for n in range(1, len(pieces)):
        lax.fori_loop(pieces[n][0], pieces[n][1], lambda c, _: (pack(c), 0)[1], 0)
        send(n)

    @pl.when(step == 0)
    def _():
        from_left[...] = jnp.zeros_like(from_left)

    @pl.when(step == time_total - 1)
    def _():
        from_right[...] = jnp.zeros_like(from_right)

    def smooth(c):
        here = pl.ds(pl.multiple_of(c * group, group), group)
        there = pl.ds(pl.multiple_of(rows - (c + 1) * group, group), group)
        left = from_left[here, :]
        right = from_right[here, :]
        for span, first, second, k in ((here, left, right, 0), (there, right, left, 1)):
            beside = jnp.where(lane, first.astype(f32), second.astype(f32)).astype(bf16)
            total = jnp.dot(field[span, :], mid[...], preferred_element_type=f32)
            total = total + jnp.dot(beside, halo[k], preferred_element_type=f32)
            weight = scales[span, :]
            pool[span, :] = (total * jnp.concatenate([weight] * (width // 128), 1)).astype(bf16)

    def across(o):
        later = 1 - (site + o) // site_total
        return pltpu.make_async_remote_copy(
            src_ref=pool.at[pl.ds(pl.multiple_of(later * (rows - group), group), group)],
            dst_ref=pool.at[pl.ds(pl.multiple_of(rows + site * group, group), group)],
            send_sem=gsend.at[o - 1],
            recv_sem=grecv.at[o - 1],
            device_id={"site": lax.rem(site + o, site_total)},
            device_id_type=MESH,
        )

    receive(0)
    smooth(0)
    for o in range(1, site_total):
        across(o).start()
    for n in range(1, len(pieces)):
        receive(n)
        lax.fori_loop(pieces[n][0], pieces[n][1], lambda c, _: (smooth(c), 0)[1], 0)

    for n in range(len(pieces)):

        @pl.when(step < time_total - 1)
        def _():
            sideways(n, True).wait_send()

        @pl.when(step > 0)
        def _():
            sideways(n, False).wait_send()

    for o in range(1, site_total):
        for copy, into, base, length, sem in (
            (points(o), geo, owned, 8, precv),
            (across(o), pool, rows, group, grecv),
        ):
            copy.wait_send()
            origin = lax.rem(site + site_total - o, site_total)
            landing = into.at[pl.ds(pl.multiple_of(base + origin * length, 8), length)]
            pltpu.make_async_remote_copy(
                src_ref=landing,
                dst_ref=landing,
                send_sem=sem.at[o - 1],
                recv_sem=sem.at[o - 1],
                device_id={"site": origin},
                device_id_type=MESH,
            ).wait_recv()


def combine_kernel(names, counts, pool, geo, scale, out, acc, tiles, across, upward, scales):
    site = lax.axis_index("site")
    blocks = scale.shape[0]
    size = tiles.shape[0]
    lanes = tiles.shape[1] // size
    width = out.shape[1]
    for ref, source in (
        (across, geo[pl.ds(0, blocks), :]),
        (upward, geo[pl.ds(blocks, blocks), :]),
        (scales, scale[...]),
    ):
        turned = jnp.transpose(source)
        for b in range(blocks):
            ref[pl.ds(b * size, size), :] = jnp.broadcast_to(turned[:, b : b + 1], (size, 128))

    def named(b, k):
        name = names[b, k]
        owner = name // blocks
        within = name - owner * blocks
        window = jnp.where(owner > site, within, within - (blocks - CAP))
        near = owner == site
        place = jnp.where(near, within, blocks + owner * CAP + window)
        first = jnp.where(near, within, 2 * blocks + 8 * owner + window)
        second = jnp.where(near, blocks + within, 2 * blocks + 8 * owner + window + CAP)
        return place, first, second

    def several(b, k):
        last = counts[b] - 1
        found = []
        for j in range(lanes):
            n = lanes * k + j
            found.append((named(b, jnp.minimum(n, last)), jnp.where(n <= last, 1.0, 0.0)))
        return found

    def build(b, k):
        for j, (slot, weight) in enumerate(several(b, k)):
            x = geo[pl.ds(slot[1], 1), :]
            y = geo[pl.ds(slot[2], 1), :]
            for r in range(0, size, 32):
                span = pl.ds(pl.multiple_of(b * size + r, 32), 32)
                dx = across[span, :] - x
                dy = upward[span, :] - y
                square = dx * dx + dy * dy
                d = square * lax.rsqrt(jnp.maximum(square, 1e-30))
                t = jnp.maximum(1.0 - d, 0.0)
                t = t * t
                value = jnp.exp2(d * (-15.0 * math.log2(math.e))) * (t * t)
                value = value * (d * (4.0 * weight) + weight)
                tiles[pl.ds(r, 32), pl.ds(j * size, size)] = value.astype(bf16)

    def multiply(b, k):
        values = jnp.concatenate(
            [pool[pl.ds(pl.multiple_of(s[0] * size, size), size), :] for s, _ in several(b, k)]
        )
        product = jnp.dot(tiles[...], values, preferred_element_type=f32)
        total = jnp.where(k > 0, acc[...], 0.0) + product
        acc[...] = total
        return total

    def finish(b, total):
        span = pl.ds(pl.multiple_of(b * size, size), size)
        weight = jnp.concatenate([scales[span, :]] * (width // 128), 1)
        out[span, :] = (total * weight).astype(bf16)

    def turns(b):
        return (counts[b] + lanes - 1) // lanes

    build(0, 0)

    def block(b, _):
        def inner(k, _):
            multiply(b, k - 1)
            build(b, k)
            return 0

        last = turns(b)
        lax.fori_loop(1, last, inner, 0)
        finish(b, multiply(b, last - 1))
        build(jnp.minimum(b + 1, blocks - 1), 0)
        return 0

    lax.fori_loop(0, blocks, block, 0)


def shards(
    site_total, time_total,
    site_field, positions, site_scale, neighbor_blocks, neighbor_count, lag_values, time_band,
):
    rows, width = site_field.shape
    blocks = neighbor_count.shape[0]
    size = rows // blocks
    reach = lag_values.shape[0] - 1
    group = CAP * size
    scale = site_scale.astype(f32).reshape(blocks, size)
    vmem = pl.BlockSpec(memory_space=pltpu.VMEM)
    smem = pl.BlockSpec(memory_space=pltpu.SMEM)
    mid, halo = pl.pallas_call(
        table_kernel,
        out_shape=[
            jax.ShapeDtypeStruct((width, width), bf16),
            jax.ShapeDtypeStruct((2, 2 * reach, width), bf16),
        ],
        in_specs=[vmem] * 2,
        out_specs=[vmem] * 2,
        scratch_shapes=[pltpu.VMEM((8, 128), f32)],
        compiler_params=pltpu.CompilerParams(vmem_limit_bytes=12 * 2**20),
        name="table",
    )(lag_values.reshape(1, -1), time_band.reshape(-1, 128))
    pool, geo = pl.pallas_call(
        functools.partial(exchange_kernel, site_total, time_total),
        out_shape=[
            jax.ShapeDtypeStruct((rows + site_total * group, width), bf16),
            jax.ShapeDtypeStruct((2 * blocks + 8 * site_total, size), f32),
        ],
        in_specs=[pl.BlockSpec(memory_space=pltpu.HBM)] + [vmem] * 4,
        out_specs=[vmem] * 2,
        scratch_shapes=[
            pltpu.VMEM((rows, width), bf16),
            pltpu.SemaphoreType.DMA,
            pltpu.VMEM((rows // 2, 128), bf16),
            pltpu.VMEM((rows // 2, 128), bf16),
            pltpu.VMEM((rows // 2, 128), bf16),
            pltpu.VMEM((rows // 2, 128), bf16),
            pltpu.VMEM((rows, 128), f32),
            pltpu.VMEM((2, 8, 128), f32),
            pltpu.SemaphoreType.DMA((2, 3)),
            pltpu.SemaphoreType.DMA((2, 3)),
            pltpu.SemaphoreType.DMA((site_total - 1,)),
            pltpu.SemaphoreType.DMA((site_total - 1,)),
            pltpu.SemaphoreType.DMA((site_total - 1,)),
            pltpu.SemaphoreType.DMA((site_total - 1,)),
        ],
        compiler_params=pltpu.CompilerParams(
            collective_id=0, has_side_effects=True, vmem_limit_bytes=24 * 2**20
        ),
        name="exchange",
    )(site_field, mid, halo, positions, scale)
    return pl.pallas_call(
        combine_kernel,
        out_shape=jax.ShapeDtypeStruct((rows, width), bf16),
        in_specs=[smem] * 2 + [vmem] * 3,
        out_specs=vmem,
        scratch_shapes=[
            pltpu.VMEM((size, width), f32),
            pltpu.VMEM((size, 6 * size), bf16),
            pltpu.VMEM((rows, 128), f32),
            pltpu.VMEM((rows, 128), f32),
            pltpu.VMEM((rows, 128), f32),
        ],
        compiler_params=pltpu.CompilerParams(vmem_limit_bytes=28 * 2**20),
        name="combine",
    )(neighbor_blocks, neighbor_count, pool, geo, scale)


def solution(mesh):
    placed = (P("site", "tm"), P(None, "site"), P("site"), P("site", None), P("site"), P(), P())
    return jax.shard_map(
        functools.partial(shards, mesh.shape["site"], mesh.shape["tm"]),
        mesh=mesh,
        in_specs=placed,
        out_specs=P("site", "tm"),
        check_vma=False,
    )
```
